512 devices in a mesh: row: 32 (over z_hi, y, core), col: 16 (over x, z_lo).
Axes of the slice: x: 4, y: 4, z: 16 (z_hi: 4, z_lo: 4; z = z_hi * 4 + z_lo), core: 2. Of those that a mesh axis runs over, the one named last changes fastest.
Arguments:
- matrix: float32 [16384, 16384], P('row', 'col'), may hold values from -4 to 4, as said below
- panel: float32 [16384, 256], P('row'), may hold values from -0.046875 to 0.046875
- tfactor: float32 [256, 256], replicated, may hold values from -1 to 2, as said below
Outputs:
- updated: float32 [16384, 16384], P('row', 'col')
The draws below stay inside these ranges and needn't reach their ends.
Inputs may be any that keep to these rules, and one draw needn't show every extreme that they name: matrix equals its transpose. tfactor is upper triangular with its diagonal in 1 to 2.
All inputs are finite; a program needn't handle non-finite values.
Results may differ from the reference program's by a relative error of at most 0.00008.
Values sent between devices are 32-bit elements; how exact they have to be, the bound alone decides.
A program may use at most 64 MiB of HBM per device.

```python
import jax
import jax.numpy as jnp
from jax import lax

K = 256
N = 16384


def draw_matrix(key, part):
    key = jax.random.fold_in(key, 11)
    base = jnp.clip(jax.random.normal(key, (N, N), jnp.float32), -4.0, 4.0)
    return (0.5 * (base + base.T)).astype(jnp.float32)


def draw_tfactor(key, part):
    key = jax.random.fold_in(key, 23)
    first, second = jax.random.split(key)
    diag_vals = jax.random.uniform(first, (K,), jnp.float32, 1.0, 2.0)
    upper = jax.random.uniform(second, (K, K), jnp.float32, -1.0, 1.0) * (3.0 * K ** (-0.5))
    upper = jnp.clip(upper, -1.0, 1.0)
    lines = jnp.arange(K, dtype=jnp.int32)
    above = lines[:, None] < lines[None, :]
    return (jnp.where(above, upper, 0.0) + jnp.diag(diag_vals)).astype(jnp.float32)


def steps_of(rng, dims, cuts, low, high):
    def one(position, blocks):
        heights = jax.random.uniform(jax.random.fold_in(jax.random.fold_in(rng, 6), position), (blocks,), jnp.float32, low / len(cuts), high / len(cuts))
        return jnp.repeat(jnp.exp(heights), dims[position] // blocks).reshape((-1,) + (1,) * (len(dims) - position - 1))

    level = one(*cuts[0])
    for cut in cuts[1:]:
        level = level * one(*cut)
    return level


def gaussian(rng, dims, scale, reach, cuts=(), kind=jnp.bfloat16):
    level = steps_of(rng, dims, cuts, -0.22, 0.18) if cuts else 1.0
    values = jax.random.normal(rng, dims, jnp.float32) * scale * level
    return jnp.minimum(jnp.maximum(values, -reach), reach).astype(kind)


def setup_inputs(seed: int = 0) -> dict:
    keys = jax.random.split(jax.random.key(seed), 4)
    return {
        "matrix": draw_matrix(jax.random.fold_in(keys[3], 71), 0),
        "panel": gaussian(keys[1], (N, K), N ** -0.5, 0.046875, ((0, 32),), jnp.float32),
        "tfactor": draw_tfactor(jax.random.fold_in(keys[3], 71), 0),
    }


def mult(left, right):
    return jnp.dot(left, right, precision=lax.Precision.HIGHEST, preferred_element_type=jnp.float32)


def reference(matrix, panel, tfactor):
    product = mult(matrix, panel)
    xmat = mult(product, tfactor)
    gram = mult(panel.T, xmat)
    wmat = xmat - 0.5 * mult(panel, mult(tfactor.T, gram))
    return matrix - mult(panel, wmat.T) - mult(wmat, panel.T)
```

```python
import functools

import jax
import jax.numpy as jnp
from jax import lax
from jax.experimental import pallas as pl
from jax.experimental.pallas import tpu as pltpu
from jax.sharding import PartitionSpec as P

MESH = pl.DeviceIdType.MESH
F32 = jnp.float32
BF16 = jnp.bfloat16
ROWS = 512
K = 256
EIGHTH = 128
SHARD = 32


def split(value):
    high = value.astype(BF16)
    return high, (value - high.astype(F32)).astype(BF16)


def dot3(left, right, contract):
    one = functools.partial(
        lax.dot_general, dimension_numbers=((contract[:1], contract[1:]), ((), ())), preferred_element_type=F32
    )
    return one(left[0], right[0]) + (one(left[0], right[1]) + one(left[1], right[0]))


def kernel(
    a_hbm, p_hbm, t_hbm, o_hbm,
    a, p, t, z, z_core, z_y, part, y_z, y_row, xj, pj, xr, q, g_part, g_in, g_sum, g_y, g_tot, g_z, g,
    load, store, core_s, core_r, p_s, p_r, y_s, y_r, py_s, py_r, zh_s, zh_r, row_s, row_r, xy_s, xy_r,
    zl_s, zl_r, rx_s, rx_r, gs_s, gs_r, gy_s, gy_r, gz_s, gz_r, ga_s, ga_r,
):
    row, col = lax.axis_index("row"), lax.axis_index("col")
    core, y, zh = row % 2, (row // 2) % 4, row // 8
    x, zl = col // 4, col % 4

    def at(x=x, y=y, zl=zl, zh=zh, core=core):
        return ((zh * 4 + y) * 2 + core, x * 4 + zl)

    def send(src, dst, s_sem, r_sem, device):
        copy = pltpu.make_async_remote_copy(src, dst, s_sem, r_sem, device_id=device, device_id_type=MESH)
        copy.start()
        return copy

    def rows(start, size):
        return pl.ds(pl.multiple_of(start, size), size)

    mod4 = lambda v: v & 3
    same = (x == y) & (y == zl) & (zl == zh)
    plane = [(dx, dc) for dx in range(4) for dc in range(2) if dx or dc]
    x_core = [at(x=mod4(x + dx), core=core ^ dc) for dx, dc in plane]
    other = at(core=1 - core)

    loads = [
        pltpu.make_async_copy(p_hbm, p, load.at[0]),
        pltpu.make_async_copy(a_hbm, a, load.at[1]),
        pltpu.make_async_copy(t_hbm, t, load.at[2]),
    ]
    for copy in loads:
        copy.start()
    barrier = pltpu.get_barrier_semaphore()

    def hello(device):
        pl.semaphore_signal(barrier, inc=1, device_id=device, device_id_type=MESH)

    for d in (2, 1, 3):
        hello(at(zh=mod4(zh + d)))
    for k in range(4):
        mine = same & (zl == k)

        @pl.when(jnp.logical_not(mine))
        def _():
            hello(at(x=y, y=zl, zl=k, zh=x))
            hello(at(x=zh, y=x, zl=y, zh=k))

    for d in (1, 2, 3):
        hello(at(zl=mod4(zl + d)))
        hello(at(y=mod4(y + d)))
    for device in x_core:
        hello(device)

    loads[0].wait()
    p_pair = split(p[...])
    loads[1].wait()

    def multiply(n, carry):
        columns = rows((((1 - core) * 2 + n) & 3) * 256, 256)
        z[columns, :] = dot3(split(a[:, columns]), p_pair, (0, 0))
        return carry

    lax.fori_loop(0, 4, multiply, 0)
    loads[2].wait()
    pl.semaphore_wait(barrier, jnp.where(same, 22, 24))

    own, theirs = rows(core * 512, 512), rows((1 - core) * 512, 512)
    waits = []
    c_z = send(z.at[theirs, :], z_core, core_s.at[0], core_r.at[0], other)
    eighth = rows(core * 512 + y * EIGHTH, EIGHTH)
    chunk = rows(x * EIGHTH, EIGHTH)

    @pl.when(jnp.logical_not(same))
    def _():
        send(p.at[chunk, :], pj.at[rows(core * 512 + x * EIGHTH, EIGHTH), :], p_s, p_r, at(x=zh, y=x, zl=y, zh=zl))

    @pl.when(same)
    def _():
        pj[eighth, :] = p[chunk, :]

    c_z.wait_recv()
    z[own, :] += z_core[...]
    c_y = []
    for d in (2, 1, 3):
        to = mod4(y + d)
        c_y.append(send(z.at[rows(core * 512 + to * EIGHTH, EIGHTH), :], z_y.at[d - 1], y_s.at[d - 1], y_r.at[d - 1], at(y=to)))
    t_pair = split(t[...])
    for copy in c_y:
        copy.wait_recv()
    part[...] = z[eighth, :] + z_y[0] + (z_y[1] + z_y[2])

    c_zh = [
        send(part, y_z.at[d - 1], zh_s.at[d - 1], zh_r.at[d - 1], at(zh=mod4(zh + d))) for d in (2, 1, 3)
    ]

    def row_copy(k, device, slot):
        return pltpu.make_async_remote_copy(
            part.at[pl.ds(k * SHARD, SHARD), :], y_row.at[slot], row_s.at[k], row_r.at[slot], device_id=device, device_id_type=MESH
        )

    for k in range(4):
        mine = same & (zl == k)

        @pl.when(jnp.logical_not(mine))
        def _():
            row_copy(k, at(x=y, y=zl, zl=k, zh=x), zh).start()

        @pl.when(mine)
        def _():
            y_row[k] = part[pl.ds(k * SHARD, SHARD), :]

    @pl.when(jnp.logical_not(same))
    def _():
        pltpu.make_async_remote_copy(
            p.at[chunk, :], pj.at[eighth, :], p_s, p_r, device_id=other, device_id_type=MESH
        ).wait()

    c_py = [
        send(pj.at[eighth, :], pj.at[eighth, :], py_s.at[d - 1], py_r.at[d - 1], at(y=mod4(y + d))) for d in (2, 1, 3)
    ]
    q[...] = dot3(p_pair, t_pair, (1, 1))
    for copy in c_py:
        copy.wait_recv()
    c_pc = send(pj.at[own, :], pj.at[own, :], core_s.at[1], core_r.at[1], other)

    for copy in c_zh:
        copy.wait_recv()
    x_own = dot3(split(part[...] + y_z[0] + (y_z[1] + y_z[2])), t_pair, (1, 0))
    xj[eighth, :] = x_own
    g_part[...] = dot3(split(pj[eighth, :]), split(x_own), (0, 0))
    mine32 = rows((x * 2 + core) * SHARD, SHARD)
    c_gs = []
    for n, (dx, dc) in enumerate(plane):
        slot = rows((mod4(x + dx) * 2 + (core ^ dc)) * SHARD, SHARD)
        c_gs.append(send(g_part.at[slot, :], g_in.at[n], gs_s.at[n], gs_r.at[n], x_core[n]))
    c_xy = [
        send(xj.at[eighth, :], xj.at[eighth, :], xy_s.at[d - 1], xy_r.at[d - 1], at(y=mod4(y + d))) for d in (2, 1, 3)
    ]

    for k in range(4):
        @pl.when(jnp.logical_not(same & (zh == k)))
        def _():
            row_copy(0, other, k).wait_recv()

    shard = rows(x * EIGHTH + zl * SHARD, SHARD)
    xr[shard, :] = dot3(split(y_row[0] + y_row[1] + (y_row[2] + y_row[3])), t_pair, (1, 0))
    c_zl = [
        send(xr.at[shard, :], xr.at[shard, :], zl_s.at[d - 1], zl_r.at[d - 1], at(zl=mod4(zl + d))) for d in (2, 1, 3)
    ]

    for copy in c_gs:
        copy.wait_recv()
    total = g_part[mine32, :]
    for n in range(7):
        total = total + g_in[n]
    g_sum[...] = total
    c_gy = [send(g_sum, g_y.at[d - 1], gy_s.at[d - 1], gy_r.at[d - 1], at(y=mod4(y + d))) for d in (2, 1, 3)]

    for copy in c_zl:
        copy.wait_recv()
    c_rx = [
        send(xr.at[chunk, :], xr.at[chunk, :], rx_s.at[d - 1], rx_r.at[d - 1], at(x=mod4(x + d))) for d in (2, 1, 3)
    ]

    for copy in c_gy:
        copy.wait_recv()
    g_tot[...] = g_sum[...] + g_y[0] + (g_y[1] + g_y[2])
    c_gz = [send(g_tot, g_z.at[d - 1], gz_s.at[d - 1], gz_r.at[d - 1], at(zl=mod4(zl + d))) for d in (2, 1, 3)]

    for copy in c_xy:
        copy.wait_recv()
    c_xc = send(xj.at[own, :], xj.at[own, :], core_s.at[2], core_r.at[2], other)

    for copy in c_gz:
        copy.wait_recv()
    g[mine32, :] = g_tot[...] + g_z[0] + (g_z[1] + g_z[2])
    c_ga = [send(g.at[mine32, :], g.at[mine32, :], ga_s.at[n], ga_r.at[n], x_core[n]) for n in range(7)]

    c_xc.wait_recv()

    def first(n, carry):
        columns = rows(n * 256, 256)
        a[:, columns] -= dot3(p_pair, split(xj[columns, :]), (1, 1))
        return carry

    lax.fori_loop(0, 4, first, 0)
    for copy in c_rx:
        copy.wait_recv()
    c_pc.wait_recv()
    for copy in c_ga:
        copy.wait_recv()
    w_pair = split(xr[...] - dot3(split(q[...]), split(g[...]), (1, 0)))

    def out(n):
        columns = rows(n * 256, 256)
        return pltpu.make_async_copy(a.at[:, columns], o_hbm.at[:, columns], store.at[n])

    def second(n, carry):
        columns = rows(n * 256, 256)
        a[:, columns] -= dot3(w_pair, split(pj[columns, :]), (1, 1))
        out(n).start()
        return carry

    lax.fori_loop(0, 4, second, 0)
    for copy in [c_z, *c_y, *c_zh, *c_py, c_pc, *c_gs, *c_xy, *c_zl, *c_gy, *c_rx, *c_gz, c_xc, *c_ga]:
        copy.wait_send()
    for k in range(4):
        @pl.when(jnp.logical_not(same & (zl == k)))
        def _():
            row_copy(k, other, 0).wait_send()

    for n in range(4):
        out(n).wait()


def per_device(matrix, panel, tfactor):
    dma = pltpu.SemaphoreType.DMA
    vmem = lambda *shape: pltpu.VMEM(shape, F32)
    return pl.pallas_call(
        kernel,
        out_shape=jax.ShapeDtypeStruct(matrix.shape, F32),
        in_specs=[pl.BlockSpec(memory_space=pl.ANY)] * 3,
        out_specs=pl.BlockSpec(memory_space=pl.ANY),
        scratch_shapes=[
            vmem(512, 1024), vmem(512, K), vmem(K, K),
            vmem(1024, K), vmem(512, K), vmem(3, EIGHTH, K), vmem(EIGHTH, K),
            vmem(3, EIGHTH, K), vmem(4, SHARD, K),
            vmem(1024, K), vmem(1024, K), vmem(512, K), vmem(512, K),
            vmem(K, K), vmem(7, SHARD, K), vmem(SHARD, K), vmem(3, SHARD, K), vmem(SHARD, K), vmem(3, SHARD, K), vmem(K, K),
            dma((3,)), dma((4,)), dma((3,)), dma((3,)), dma, dma, dma((3,)), dma((3,)), dma((3,)), dma((3,)),
            dma((3,)), dma((3,)), dma((4,)), dma((4,)), dma((3,)), dma((3,)),
            dma((3,)), dma((3,)), dma((3,)), dma((3,)), dma((7,)), dma((7,)), dma((3,)), dma((3,)),
            dma((3,)), dma((3,)), dma((7,)), dma((7,)),
        ],
        compiler_params=pltpu.CompilerParams(collective_id=0, has_side_effects=True, vmem_limit_bytes=40 * 2**20),
    )(matrix, panel, tfactor)


def solution(mesh):
    return jax.shard_map(
        per_device,
        mesh=mesh,
        in_specs=(P("row", "col"), P("row", None), P()),
        out_specs=P("row", "col"),
        check_vma=False,
    )
```

```python
import functools

import jax
import jax.numpy as jnp
from jax import lax
from jax.experimental import pallas as pl
from jax.experimental.pallas import tpu as pltpu
from jax.sharding import PartitionSpec as P

MESH = pl.DeviceIdType.MESH
F32 = jnp.float32
BF16 = jnp.bfloat16
ROWS = 512
K = 256
EIGHTH = 128
SHARD = 32


def split(value):
    high = value.astype(BF16)
    return high, (value - high.astype(F32)).astype(BF16)


def dot3(left, right, contract):
    one = functools.partial(
        lax.dot_general, dimension_numbers=((contract[:1], contract[1:]), ((), ())), preferred_element_type=F32
    )
    return one(left[0], right[0]) + (one(left[0], right[1]) + one(left[1], right[0]))


def kernel(
    a_hbm, p_hbm, t_hbm, o_hbm,
    a, p, t, z, z_core, z_y, part, pair, y_z, xj, pj, xr, q, g_part, g_in, g_sum, g_y, g_tot, g_z, g,
    load, store, core_s, core_r, p_s, p_r, y_s, y_r, py_s, py_r, zh_s, zh_r, row_s, row_r, xy_s, xy_r,
    zl_s, zl_r, rx_s, rx_r, gs_s, gs_r, gy_s, gy_r, gz_s, gz_r, ga_s, ga_r,
):
    row, col = lax.axis_index("row"), lax.axis_index("col")
    core, y, zh = row % 2, (row // 2) % 4, row // 8
    x, zl = col // 4, col % 4

    def at(x=x, y=y, zl=zl, zh=zh, core=core):
        return ((zh * 4 + y) * 2 + core, x * 4 + zl)

    def send(src, dst, s_sem, r_sem, device):
        copy = pltpu.make_async_remote_copy(src, dst, s_sem, r_sem, device_id=device, device_id_type=MESH)
        copy.start()
        return copy

    def rows(start, size):
        return pl.ds(pl.multiple_of(start, size), size)

    mod4 = lambda v: v & 3
    same = (x == y) & (y == zl) & (zl == zh)
    plane = [(dx, dc) for dx in range(4) for dc in range(2) if dx or dc]
    x_core = [at(x=mod4(x + dx), core=core ^ dc) for dx, dc in plane]
    other = at(core=1 - core)

    loads = [
        pltpu.make_async_copy(p_hbm, p, load.at[0]),
        pltpu.make_async_copy(a_hbm, a, load.at[1]),
        pltpu.make_async_copy(t_hbm, t, load.at[2]),
    ]
    for copy in loads:
        copy.start()
    barrier = pltpu.get_barrier_semaphore()

    def hello(device):
        pl.semaphore_signal(barrier, inc=1, device_id=device, device_id_type=MESH)

    pairs = (at(zh=zh ^ 1), at(zh=zh ^ 3))
    onward, back = at(x=zh, y=x, zl=y, zh=zl), at(x=y, y=zl, zl=zh, zh=x)

    @pl.when(jnp.logical_not(same))
    def _():
        hello(onward)
        hello(back)

    for device in pairs:
        hello(device)
    for d in (1, 2, 3):
        hello(at(zl=mod4(zl + d)))
        hello(at(y=mod4(y + d)))
    for device in x_core:
        hello(device)

    loads[0].wait()
    p_pair = split(p[...])
    loads[1].wait()

    def multiply(n, carry):
        columns = rows((((1 - core) * 2 + n) & 3) * 256, 256)
        z[columns, :] = dot3(split(a[:, columns]), p_pair, (0, 0))
        return carry

    lax.fori_loop(0, 4, multiply, 0)
    loads[2].wait()
    pl.semaphore_wait(barrier, jnp.where(same, 15, 17))

    own, theirs = rows(core * 512, 512), rows((1 - core) * 512, 512)
    c_z = send(z.at[theirs, :], z_core, core_s.at[0], core_r.at[0], other)
    eighth = rows(core * 512 + y * EIGHTH, EIGHTH)
    chunk = rows(x * EIGHTH, EIGHTH)

    @pl.when(jnp.logical_not(same))
    def _():
        send(p.at[chunk, :], pj.at[rows(core * 512 + x * EIGHTH, EIGHTH), :], p_s, p_r, onward)

    @pl.when(same)
    def _():
        pj[eighth, :] = p[chunk, :]

    c_z.wait_recv()
    z[own, :] += z_core[...]
    c_y = []
    for d in (2, 1, 3):
        to = mod4(y + d)
        c_y.append(send(z.at[rows(core * 512 + to * EIGHTH, EIGHTH), :], z_y.at[d - 1], y_s.at[d - 1], y_r.at[d - 1], at(y=to)))
    t_pair = split(t[...])
    for copy in c_y:
        copy.wait_recv()
    part[...] = z[eighth, :] + z_y[0] + (z_y[1] + z_y[2])

    half = [pl.ds(0, EIGHTH // 2), pl.ds(EIGHTH // 2, EIGHTH // 2)]
    c_z1 = [send(part.at[half[h], :], y_z.at[h], zh_s.at[h], zh_r.at[h], pairs[h]) for h in range(2)]

    @pl.when(jnp.logical_not(same))
    def _():
        pltpu.make_async_remote_copy(
            p.at[chunk, :], pj.at[eighth, :], p_s, p_r, device_id=other, device_id_type=MESH
        ).wait()

    c_py = [
        send(pj.at[eighth, :], pj.at[eighth, :], py_s.at[d - 1], py_r.at[d - 1], at(y=mod4(y + d))) for d in (2, 1, 3)
    ]
    q[...] = dot3(p_pair, t_pair, (1, 1))
    for copy in c_py:
        copy.wait_recv()
    c_pc = send(pj.at[own, :], pj.at[own, :], core_s.at[1], core_r.at[1], other)

    c_z2 = []
    for h in range(2):
        c_z1[h].wait_recv()
        pair[half[h], :] = part[half[h], :] + y_z[h]
        c_z2.append(send(pair.at[half[h], :], y_z.at[2 + h], zh_s.at[2 + h], zh_r.at[2 + h], pairs[1 - h]))
    for copy in c_z2:
        copy.wait_recv()
    x_own = dot3(split(pair[...] + jnp.concatenate([y_z[2], y_z[3]], axis=0)), t_pair, (1, 0))
    xj[eighth, :] = x_own
    piece = rows(core * 512 + y * EIGHTH + zh * SHARD, SHARD)
    row_shard = lambda first, second: rows(first * EIGHTH + second * SHARD, SHARD)
    shard = row_shard(x, zl)

    @pl.when(jnp.logical_not(same))
    def _():
        send(xj.at[piece, :], xr.at[row_shard(y, zh), :], row_s, row_r, back)

    @pl.when(same)
    def _():
        xr[shard, :] = xj[piece, :]

    g_part[...] = dot3(split(pj[eighth, :]), split(x_own), (0, 0))
    mine32 = rows((x * 2 + core) * SHARD, SHARD)
    c_gs = []
    for n, (dx, dc) in enumerate(plane):
        slot = rows((mod4(x + dx) * 2 + (core ^ dc)) * SHARD, SHARD)
        c_gs.append(send(g_part.at[slot, :], g_in.at[n], gs_s.at[n], gs_r.at[n], x_core[n]))
    c_xy = [
        send(xj.at[eighth, :], xj.at[eighth, :], xy_s.at[d - 1], xy_r.at[d - 1], at(y=mod4(y + d))) for d in (2, 1, 3)
    ]

    @pl.when(jnp.logical_not(same))
    def _():
        pltpu.make_async_remote_copy(
            xj.at[piece, :], xr.at[shard, :], row_s, row_r, device_id=other, device_id_type=MESH
        ).wait()

    c_zl = [
        send(xr.at[shard, :], xr.at[shard, :], zl_s.at[d - 1], zl_r.at[d - 1], at(zl=mod4(zl + d))) for d in (2, 1, 3)
    ]

    for copy in c_gs:
        copy.wait_recv()
    total = g_part[mine32, :]
    for n in range(7):
        total = total + g_in[n]
    g_sum[...] = total
    c_gy = [send(g_sum, g_y.at[d - 1], gy_s.at[d - 1], gy_r.at[d - 1], at(y=mod4(y + d))) for d in (2, 1, 3)]

    for copy in c_zl:
        copy.wait_recv()
    c_rx = [
        send(xr.at[chunk, :], xr.at[chunk, :], rx_s.at[d - 1], rx_r.at[d - 1], at(x=mod4(x + d))) for d in (2, 1, 3)
    ]

    for copy in c_gy:
        copy.wait_recv()
    g_tot[...] = g_sum[...] + g_y[0] + (g_y[1] + g_y[2])
    c_gz = [send(g_tot, g_z.at[d - 1], gz_s.at[d - 1], gz_r.at[d - 1], at(zl=mod4(zl + d))) for d in (2, 1, 3)]

    for copy in c_xy:
        copy.wait_recv()
    c_xc = send(xj.at[own, :], xj.at[own, :], core_s.at[2], core_r.at[2], other)

    for copy in c_gz:
        copy.wait_recv()
    g[mine32, :] = g_tot[...] + g_z[0] + (g_z[1] + g_z[2])
    c_ga = [send(g.at[mine32, :], g.at[mine32, :], ga_s.at[n], ga_r.at[n], x_core[n]) for n in range(7)]

    c_xc.wait_recv()

    def first(n, carry):
        columns = rows(n * 256, 256)
        a[:, columns] -= dot3(p_pair, split(xj[columns, :]), (1, 1))
        return carry

    lax.fori_loop(0, 4, first, 0)
    for copy in c_rx:
        copy.wait_recv()
    c_pc.wait_recv()
    for copy in c_ga:
        copy.wait_recv()
    w_pair = split(xr[...] - dot3(split(q[...]), split(g[...]), (1, 0)))

    def out(n):
        columns = rows(n * 256, 256)
        return pltpu.make_async_copy(a.at[:, columns], o_hbm.at[:, columns], store.at[n])

    def second(n, carry):
        columns = rows(n * 256, 256)
        a[:, columns] -= dot3(w_pair, split(pj[columns, :]), (1, 1))
        out(n).start()
        return carry

    lax.fori_loop(0, 4, second, 0)
    for copy in [c_z, *c_y, *c_z1, *c_z2, *c_py, c_pc, *c_gs, *c_xy, *c_zl, *c_gy, *c_rx, *c_gz, c_xc, *c_ga]:
        copy.wait_send()
    for n in range(4):
        out(n).wait()


def per_device(matrix, panel, tfactor):
    dma = pltpu.SemaphoreType.DMA
    vmem = lambda *shape: pltpu.VMEM(shape, F32)
    return pl.pallas_call(
        kernel,
        out_shape=jax.ShapeDtypeStruct(matrix.shape, F32),
        in_specs=[pl.BlockSpec(memory_space=pl.ANY)] * 3,
        out_specs=pl.BlockSpec(memory_space=pl.ANY),
        scratch_shapes=[
            vmem(512, 1024), vmem(512, K), vmem(K, K),
            vmem(1024, K), vmem(512, K), vmem(3, EIGHTH, K), vmem(EIGHTH, K),
            vmem(EIGHTH, K), vmem(4, EIGHTH // 2, K),
            vmem(1024, K), vmem(1024, K), vmem(512, K), vmem(512, K),
            vmem(K, K), vmem(7, SHARD, K), vmem(SHARD, K), vmem(3, SHARD, K), vmem(SHARD, K), vmem(3, SHARD, K), vmem(K, K),
            dma((3,)), dma((4,)), dma((3,)), dma((3,)), dma, dma, dma((3,)), dma((3,)), dma((3,)), dma((3,)),
            dma((4,)), dma((4,)), dma, dma, dma((3,)), dma((3,)),
            dma((3,)), dma((3,)), dma((3,)), dma((3,)), dma((7,)), dma((7,)), dma((3,)), dma((3,)),
            dma((3,)), dma((3,)), dma((7,)), dma((7,)),
        ],
        compiler_params=pltpu.CompilerParams(collective_id=0, has_side_effects=True, vmem_limit_bytes=62 * 2**20),
    )(matrix, panel, tfactor)


def solution(mesh):
    return jax.shard_map(
        per_device,
        mesh=mesh,
        in_specs=(P("row", "col"), P("row", None), P()),
        out_specs=P("row", "col"),
        check_vma=False,
    )
```

```python
import functools

import jax
import jax.numpy as jnp
from jax import lax
from jax.experimental import pallas as pl
from jax.experimental.pallas import tpu as pltpu
from jax.sharding import PartitionSpec as P

MESH = pl.DeviceIdType.MESH
F32 = jnp.float32
BF16 = jnp.bfloat16
ROWS = 512
K = 256
EIGHTH = 128
SHARD = 32


def split(value):
    high = value.astype(BF16)
    return high, (value - high.astype(F32)).astype(BF16)


def dot3(left, right, contract):
    one = functools.partial(
        lax.dot_general, dimension_numbers=((contract[:1], contract[1:]), ((), ())), preferred_element_type=F32
    )
    return one(left[0], right[0]) + (one(left[0], right[1]) + one(left[1], right[0]))


def kernel(
    a_hbm, p_hbm, t_hbm, o_hbm,
    a, p, t, z, z_core, z_y, part, pair, y_z, xj, pj, pj_high, pj_low, r_part, r_x, r_sum, r_z, xr, q,
    g_part, g_in, g_sum, g_y, g_tot, g_z, g_block, g_zh, g_pair, g,
    load, store, core_s, core_r, p_s, p_r, y_s, y_r, py_s, py_r, zh_s, zh_r, xy_s, xy_r, zl_s, zl_r, rx_s, rx_r,
    r1_s, r1_r, r2_s, r2_r, gs_s, gs_r, gy_s, gy_r, gz_s, gz_r, gh_s, gh_r, ga_s, ga_r,
):
    row, col = lax.axis_index("row"), lax.axis_index("col")
    core, y, zh = row % 2, (row // 2) % 4, row // 8
    x, zl = col // 4, col % 4

    def at(x=x, y=y, zl=zl, zh=zh, core=core):
        return ((zh * 4 + y) * 2 + core, x * 4 + zl)

    def send(src, dst, s_sem, r_sem, device):
        copy = pltpu.make_async_remote_copy(src, dst, s_sem, r_sem, device_id=device, device_id_type=MESH)
        copy.start()
        return copy

    def rows(start, size):
        return pl.ds(pl.multiple_of(start, size), size)

    mod4 = lambda v: v & 3
    same = (x == y) & (y == zl) & (zl == zh)
    plane = [(dx, dc) for dx in range(4) for dc in range(2) if dx or dc]
    x_core = [at(x=mod4(x + dx), core=core ^ dc) for dx, dc in plane]
    other = at(core=1 - core)

    loads = [
        pltpu.make_async_copy(p_hbm, p, load.at[0]),
        pltpu.make_async_copy(a_hbm, a, load.at[1]),
        pltpu.make_async_copy(t_hbm, t, load.at[2]),
    ]
    for copy in loads:
        copy.start()
    barrier = pltpu.get_barrier_semaphore()

    def hello(device):
        pl.semaphore_signal(barrier, inc=1, device_id=device, device_id_type=MESH)

    pairs = (at(zh=zh ^ 1), at(zh=zh ^ 3))
    onward, back = at(x=zh, y=x, zl=y, zh=zl), at(x=y, y=zl, zl=zh, zh=x)

    @pl.when(jnp.logical_not(same))
    def _():
        hello(onward)
        hello(back)

    for device in pairs:
        hello(device)
    for d in (1, 2, 3):
        hello(at(zl=mod4(zl + d)))
        hello(at(y=mod4(y + d)))
    for device in x_core:
        hello(device)

    loads[0].wait()
    p_pair = split(p[...])
    loads[1].wait()

    def multiply(n, carry):
        columns = rows((((1 - core) * 2 + n) & 3) * 256, 256)
        z[columns, :] = dot3(split(a[:, columns]), p_pair, (0, 0))
        return carry

    lax.fori_loop(0, 4, multiply, 0)
    loads[2].wait()
    pl.semaphore_wait(barrier, jnp.where(same, 15, 17))

    own, theirs = rows(core * 512, 512), rows((1 - core) * 512, 512)
    c_z = send(z.at[theirs, :], z_core, core_s.at[0], core_r.at[0], other)
    eighth = rows(core * 512 + y * EIGHTH, EIGHTH)
    chunk = rows(x * EIGHTH, EIGHTH)

    @pl.when(jnp.logical_not(same))
    def _():
        send(p.at[chunk, :], pj.at[rows(core * 512 + x * EIGHTH, EIGHTH), :], p_s, p_r, onward)

    @pl.when(same)
    def _():
        pj[eighth, :] = p[chunk, :]

    c_z.wait_recv()
    z[own, :] += z_core[...]
    c_y = []
    for d in (2, 1, 3):
        to = mod4(y + d)
        c_y.append(send(z.at[rows(core * 512 + to * EIGHTH, EIGHTH), :], z_y.at[d - 1], y_s.at[d - 1], y_r.at[d - 1], at(y=to)))
    t_pair = split(t[...])
    q[...] = dot3(p_pair, t_pair, (1, 1))

    def gather(array, s_sem, r_sem, c_slot):
        moves = [send(array.at[eighth, :], array.at[eighth, :], core_s.at[c_slot], core_r.at[c_slot], other)]
        along = {
            d: send(array.at[eighth, :], array.at[eighth, :], s_sem.at[d - 1], r_sem.at[d - 1], at(y=mod4(y + d)))
            for d in (2, 1, 3)
        }

        def forward():
            for d in (1, 3, 2):
                along[d].wait_recv()
                lines = rows(core * 512 + mod4(y - d) * EIGHTH, EIGHTH)
                moves.append(send(array.at[lines, :], array.at[lines, :], core_s.at[c_slot + d], core_r.at[c_slot + d], other))

        return moves, list(along.values()), forward

    for copy in c_y:
        copy.wait_recv()
    part[...] = z[eighth, :] + z_y[0] + (z_y[1] + z_y[2])
    half = [pl.ds(0, EIGHTH // 2), pl.ds(EIGHTH // 2, EIGHTH // 2)]
    c_z1 = [send(part.at[half[h], :], y_z.at[h], zh_s.at[h], zh_r.at[h], pairs[h]) for h in range(2)]

    @pl.when(jnp.logical_not(same))
    def _():
        pltpu.make_async_remote_copy(
            p.at[chunk, :], pj.at[eighth, :], p_s, p_r, device_id=other, device_id_type=MESH
        ).wait()

    c_pc, c_py, forward_p = gather(pj, py_s, py_r, 1)
    g_part[...] = dot3(split(pj[eighth, :]), split(part[...]), (0, 0))
    mine32 = rows((x * 2 + core) * SHARD, SHARD)
    c_gs = []
    for n, (dx, dc) in enumerate(plane):
        slot = rows((mod4(x + dx) * 2 + (core ^ dc)) * SHARD, SHARD)
        c_gs.append(send(g_part.at[slot, :], g_in.at[n], gs_s.at[n], gs_r.at[n], x_core[n]))

    c_z2 = []
    for h in range(2):
        c_z1[h].wait_recv()
        pair[half[h], :] = part[half[h], :] + y_z[h]
        c_z2.append(send(pair.at[half[h], :], y_z.at[2 + h], zh_s.at[2 + h], zh_r.at[2 + h], pairs[1 - h]))

    for copy in c_gs:
        copy.wait_recv()
    total = g_part[mine32, :]
    for n in range(7):
        total = total + g_in[n]
    g_sum[...] = total
    c_gy = [send(g_sum, g_y.at[d - 1], gy_s.at[d - 1], gy_r.at[d - 1], at(y=mod4(y + d))) for d in (2, 1, 3)]

    forward_p()
    for copy in c_pc:
        copy.wait_recv()
    high, low = split(pj[...])
    pj_high[...] = high
    pj_low[...] = low
    r_part[...] = jnp.zeros_like(r_part)

    def row_product(n, carry):
        columns = rows(n * 256, 256)
        r_part[...] += dot3(split(a[:, columns]), (pj_high[columns, :], pj_low[columns, :]), (1, 0))
        return carry

    lax.fori_loop(0, 4, row_product, 0)
    c_r1 = []
    for d in (2, 1, 3):
        to = mod4(x + d)
        c_r1.append(send(r_part.at[rows(to * EIGHTH, EIGHTH), :], r_x.at[d - 1], r1_s.at[d - 1], r1_r.at[d - 1], at(x=to)))

    for copy in c_gy:
        copy.wait_recv()
    g_tot[...] = g_sum[...] + g_y[0] + (g_y[1] + g_y[2])
    c_gz = [send(g_tot, g_z.at[d - 1], gz_s.at[d - 1], gz_r.at[d - 1], at(zl=mod4(zl + d))) for d in (2, 1, 3)]

    for copy in c_z2:
        copy.wait_recv()
    xj[eighth, :] = dot3(split(pair[...] + jnp.concatenate([y_z[2], y_z[3]], axis=0)), t_pair, (1, 0))
    c_xc, c_xy, forward_x = gather(xj, xy_s, xy_r, 5)

    for copy in c_gz:
        copy.wait_recv()
    g_block[...] = g_tot[...] + g_z[0] + (g_z[1] + g_z[2])
    small = [pl.ds(0, SHARD // 2), pl.ds(SHARD // 2, SHARD // 2)]
    c_g1 = [send(g_block.at[small[h], :], g_zh.at[h], gh_s.at[h], gh_r.at[h], pairs[h]) for h in range(2)]

    for copy in c_r1:
        copy.wait_recv()
    r_sum[...] = r_part[chunk, :] + r_x[0] + (r_x[1] + r_x[2])
    c_r2 = []
    for d in (2, 1, 3):
        to = mod4(zl + d)
        c_r2.append(send(r_sum.at[rows(to * SHARD, SHARD), :], r_z.at[d - 1], r2_s.at[d - 1], r2_r.at[d - 1], at(zl=to)))

    c_g2 = []
    for h in range(2):
        c_g1[h].wait_recv()
        g_pair[small[h], :] = g_block[small[h], :] + g_zh[h]
        c_g2.append(send(g_pair.at[small[h], :], g_zh.at[2 + h], gh_s.at[2 + h], gh_r.at[2 + h], pairs[1 - h]))

    for copy in c_r2:
        copy.wait_recv()
    shard = rows(x * EIGHTH + zl * SHARD, SHARD)
    xr[shard, :] = dot3(split(r_sum[rows(zl * SHARD, SHARD), :] + r_z[0] + (r_z[1] + r_z[2])), t_pair, (1, 0))
    c_zl = [
        send(xr.at[shard, :], xr.at[shard, :], zl_s.at[d - 1], zl_r.at[d - 1], at(zl=mod4(zl + d))) for d in (2, 1, 3)
    ]

    forward_x()

    for copy in c_g2:
        copy.wait_recv()
    g[mine32, :] = g_pair[...] + jnp.concatenate([g_zh[2], g_zh[3]], axis=0)
    c_ga = [send(g.at[mine32, :], g.at[mine32, :], ga_s.at[n], ga_r.at[n], x_core[n]) for n in range(7)]

    for copy in c_zl:
        copy.wait_recv()
    c_rx = [
        send(xr.at[chunk, :], xr.at[chunk, :], rx_s.at[d - 1], rx_r.at[d - 1], at(x=mod4(x + d))) for d in (2, 1, 3)
    ]

    for copy in c_xc:
        copy.wait_recv()

    def first(n, carry):
        columns = rows(n * 256, 256)
        a[:, columns] -= dot3(p_pair, split(xj[columns, :]), (1, 1))
        return carry

    lax.fori_loop(0, 4, first, 0)
    for copy in c_ga:
        copy.wait_recv()
    q[...] = dot3(split(q[...]), split(dot3(split(g[...]), t_pair, (1, 0))), (1, 0))
    for copy in c_rx:
        copy.wait_recv()
    w_pair = split(xr[...] - q[...])

    def out(n):
        columns = rows(n * 256, 256)
        return pltpu.make_async_copy(a.at[:, columns], o_hbm.at[:, columns], store.at[n])

    def second(n, carry):
        columns = rows(n * 256, 256)
        a[:, columns] -= dot3(w_pair, (pj_high[columns, :], pj_low[columns, :]), (1, 1))
        out(n).start()
        return carry

    lax.fori_loop(0, 4, second, 0)
    for copy in [c_z, *c_y, *c_z1, *c_z2, *c_py, *c_pc, *c_gs, *c_xy, *c_zl, *c_gy, *c_rx, *c_gz, *c_xc, *c_ga, *c_r1, *c_r2, *c_g1, *c_g2]:
        copy.wait_send()
    for n in range(4):
        out(n).wait()


def per_device(matrix, panel, tfactor):
    dma = pltpu.SemaphoreType.DMA
    vmem = lambda *shape: pltpu.VMEM(shape, F32)
    return pl.pallas_call(
        kernel,
        out_shape=jax.ShapeDtypeStruct(matrix.shape, F32),
        in_specs=[pl.BlockSpec(memory_space=pltpu.HBM)] * 3,
        out_specs=pl.BlockSpec(memory_space=pl.ANY),
        scratch_shapes=[
            vmem(512, 1024), vmem(512, K), vmem(K, K),
            vmem(1024, K), vmem(512, K), vmem(3, EIGHTH, K), vmem(EIGHTH, K), vmem(EIGHTH, K), vmem(4, EIGHTH // 2, K),
            vmem(1024, K), vmem(1024, K), pltpu.VMEM((1024, K), BF16), pltpu.VMEM((1024, K), BF16),
            vmem(512, K), vmem(3, EIGHTH, K), vmem(EIGHTH, K), vmem(3, SHARD, K), vmem(512, K), vmem(512, K),
            vmem(K, K), vmem(7, SHARD, K), vmem(SHARD, K), vmem(3, SHARD, K), vmem(SHARD, K), vmem(3, SHARD, K),
            vmem(SHARD, K), vmem(4, SHARD // 2, K), vmem(SHARD, K), vmem(K, K),
            dma((3,)), dma((4,)), dma((9,)), dma((9,)), dma, dma, dma((3,)), dma((3,)), dma((3,)), dma((3,)),
            dma((4,)), dma((4,)), dma((3,)), dma((3,)), dma((3,)), dma((3,)), dma((3,)), dma((3,)),
            dma((3,)), dma((3,)), dma((3,)), dma((3,)), dma((7,)), dma((7,)), dma((3,)), dma((3,)),
            dma((3,)), dma((3,)), dma((4,)), dma((4,)), dma((7,)), dma((7,)),
        ],
        compiler_params=pltpu.CompilerParams(collective_id=0, has_side_effects=True, vmem_limit_bytes=62 * 2**20),
    )(matrix, panel, tfactor)


def solution(mesh):
    return jax.shard_map(
        per_device,
        mesh=mesh,
        in_specs=(P("row", "col"), P("row", None), P()),
        out_specs=P("row", "col"),
        check_vma=False,
    )
```

```python
import functools

import jax
import jax.numpy as jnp
from jax import lax
from jax.experimental import pallas as pl
from jax.experimental.pallas import tpu as pltpu
from jax.sharding import PartitionSpec as P

MESH = pl.DeviceIdType.MESH
F32 = jnp.float32
BF16 = jnp.bfloat16
ROWS = 512
K = 256
EIGHTH = 128
SHARD = 32


def split(value):
    high = value.astype(BF16)
    return high, (value - high.astype(F32)).astype(BF16)


def dot3(left, right, contract):
    one = functools.partial(
        lax.dot_general, dimension_numbers=((contract[:1], contract[1:]), ((), ())), preferred_element_type=F32
    )
    return one(left[0], right[0]) + (one(left[0], right[1]) + one(left[1], right[0]))


def kernel(
    a_hbm, p_hbm, t_hbm, o_hbm,
    a, p, t, z, z_core, z_y, part, pair, y_z, xj, pj, pj_high, pj_low, r_part, r_x, r_sum, r_z, xr, q,
    g_part, g_core, g_in, g_sum, g_y, g_tot, g_z, g_block, g_zh, g_pair, g,
    load, store, core_s, core_r, p_s, p_r, y_s, y_r, py_s, py_r, zh_s, zh_r, xy_s, xy_r, zl_s, zl_r, rx_s, rx_r,
    r1_s, r1_r, r2_s, r2_r, gs_s, gs_r, gy_s, gy_r, gz_s, gz_r, gh_s, gh_r, ga_s, ga_r, gc_s, gc_r,
):
    row, col = lax.axis_index("row"), lax.axis_index("col")
    core, y, zh = row % 2, (row // 2) % 4, row // 8
    x, zl = col // 4, col % 4

    def at(x=x, y=y, zl=zl, zh=zh, core=core):
        return ((zh * 4 + y) * 2 + core, x * 4 + zl)

    def send(src, dst, s_sem, r_sem, device):
        copy = pltpu.make_async_remote_copy(src, dst, s_sem, r_sem, device_id=device, device_id_type=MESH)
        copy.start()
        return copy

    def rows(start, size):
        return pl.ds(pl.multiple_of(start, size), size)

    mod4 = lambda v: v & 3
    same = (x == y) & (y == zl) & (zl == zh)
    other = at(core=1 - core)

    loads = [
        pltpu.make_async_copy(p_hbm, p, load.at[0]),
        pltpu.make_async_copy(a_hbm, a, load.at[1]),
        pltpu.make_async_copy(t_hbm, t, load.at[2]),
    ]
    for copy in loads:
        copy.start()
    barrier = pltpu.get_barrier_semaphore()

    def hello(device):
        pl.semaphore_signal(barrier, inc=1, device_id=device, device_id_type=MESH)

    pairs = (at(zh=zh ^ 1), at(zh=zh ^ 3))
    onward, back = at(x=zh, y=x, zl=y, zh=zl), at(x=y, y=zl, zl=zh, zh=x)

    @pl.when(jnp.logical_not(same))
    def _():
        hello(onward)
        hello(back)

    for device in pairs:
        hello(device)
    for d in (1, 2, 3):
        hello(at(zl=mod4(zl + d)))
        hello(at(y=mod4(y + d)))
    hello(other)
    for d in (1, 2, 3):
        hello(at(x=mod4(x + d)))

    loads[0].wait()
    p_pair = split(p[...])
    loads[1].wait()

    def multiply(n, carry):
        columns = rows((((1 - core) * 2 + n) & 3) * 256, 256)
        z[columns, :] = dot3(split(a[:, columns]), p_pair, (0, 0))
        return carry

    lax.fori_loop(0, 4, multiply, 0)
    loads[2].wait()
    pl.semaphore_wait(barrier, jnp.where(same, 12, 14))

    own, theirs = rows(core * 512, 512), rows((1 - core) * 512, 512)
    c_z = send(z.at[theirs, :], z_core, core_s.at[0], core_r.at[0], other)
    eighth = rows(core * 512 + y * EIGHTH, EIGHTH)
    chunk = rows(x * EIGHTH, EIGHTH)

    @pl.when(jnp.logical_not(same))
    def _():
        send(p.at[chunk, :], pj.at[rows(core * 512 + x * EIGHTH, EIGHTH), :], p_s, p_r, onward)

    @pl.when(same)
    def _():
        pj[eighth, :] = p[chunk, :]

    c_z.wait_recv()
    z[own, :] += z_core[...]
    c_y = []
    for d in (2, 1, 3):
        to = mod4(y + d)
        c_y.append(send(z.at[rows(core * 512 + to * EIGHTH, EIGHTH), :], z_y.at[d - 1], y_s.at[d - 1], y_r.at[d - 1], at(y=to)))
    t_pair = split(t[...])
    q_pair = split(dot3(p_pair, t_pair, (1, 1)))

    def gather(array, s_sem, r_sem, c_slot):
        moves = [send(array.at[eighth, :], array.at[eighth, :], core_s.at[c_slot], core_r.at[c_slot], other)]
        along = {
            d: send(array.at[eighth, :], array.at[eighth, :], s_sem.at[d - 1], r_sem.at[d - 1], at(y=mod4(y + d)))
            for d in (2, 1, 3)
        }

        def forward():
            for d in (1, 3, 2):
                along[d].wait_recv()
                lines = rows(core * 512 + mod4(y - d) * EIGHTH, EIGHTH)
                moves.append(send(array.at[lines, :], array.at[lines, :], core_s.at[c_slot + d], core_r.at[c_slot + d], other))

        return moves, list(along.values()), forward

    for copy in c_y:
        copy.wait_recv()
    part[...] = dot3(split(z[eighth, :] + z_y[0] + (z_y[1] + z_y[2])), t_pair, (1, 0))
    half = [pl.ds(0, EIGHTH // 2), pl.ds(EIGHTH // 2, EIGHTH // 2)]
    c_z1 = [send(part.at[half[h], :], y_z.at[h], zh_s.at[h], zh_r.at[h], pairs[h]) for h in range(2)]

    @pl.when(jnp.logical_not(same))
    def _():
        pltpu.make_async_remote_copy(
            p.at[chunk, :], pj.at[eighth, :], p_s, p_r, device_id=other, device_id_type=MESH
        ).wait()

    c_pc, c_py, forward_p = gather(pj, py_s, py_r, 1)
    g_part[...] = dot3(split(pj[eighth, :]), split(part[...]), (0, 0))
    my64, their64 = rows(core * 128, 128), rows((1 - core) * 128, 128)
    mine32 = rows(core * 128 + x * SHARD, SHARD)
    c_gc = send(g_part.at[their64, :], g_core, gc_s.at[0], gc_r.at[0], other)
    c_gc.wait_recv()
    g_part[my64, :] += g_core[...]
    c_gs = []
    for d in (2, 1, 3):
        to = mod4(x + d)
        c_gs.append(send(g_part.at[rows(core * 128 + to * SHARD, SHARD), :], g_in.at[d - 1], gs_s.at[d - 1], gs_r.at[d - 1], at(x=to)))

    c_z2 = []
    for h in range(2):
        c_z1[h].wait_recv()
        pair[half[h], :] = part[half[h], :] + y_z[h]
        c_z2.append(send(pair.at[half[h], :], y_z.at[2 + h], zh_s.at[2 + h], zh_r.at[2 + h], pairs[1 - h]))

    for copy in c_gs:
        copy.wait_recv()
    total = g_part[mine32, :]
    for n in range(3):
        total = total + g_in[n]
    g_sum[...] = total
    c_gy = [send(g_sum, g_y.at[d - 1], gy_s.at[d - 1], gy_r.at[d - 1], at(y=mod4(y + d))) for d in (2, 1, 3)]

    forward_p()
    for copy in c_pc:
        copy.wait_recv()
    high, low = split(pj[...])
    pj_high[...] = high
    pj_low[...] = low
    r_part[...] = jnp.zeros_like(r_part)

    def row_product(n, carry):
        columns = rows(n * 256, 256)
        r_part[...] += dot3(split(a[:, columns]), (pj_high[columns, :], pj_low[columns, :]), (1, 0))
        return carry

    lax.fori_loop(0, 4, row_product, 0)
    c_r1 = []
    for d in (2, 1, 3):
        to = mod4(x + d)
        c_r1.append(send(r_part.at[rows(to * EIGHTH, EIGHTH), :], r_x.at[d - 1], r1_s.at[d - 1], r1_r.at[d - 1], at(x=to)))

    for copy in c_gy:
        copy.wait_recv()
    g_tot[...] = g_sum[...] + g_y[0] + (g_y[1] + g_y[2])
    c_gz = [send(g_tot, g_z.at[d - 1], gz_s.at[d - 1], gz_r.at[d - 1], at(zl=mod4(zl + d))) for d in (2, 1, 3)]

    for copy in c_gz:
        copy.wait_recv()
    g_block[...] = g_tot[...] + g_z[0] + (g_z[1] + g_z[2])
    small = [pl.ds(0, SHARD // 2), pl.ds(SHARD // 2, SHARD // 2)]
    c_g1 = [send(g_block.at[small[h], :], g_zh.at[h], gh_s.at[h], gh_r.at[h], pairs[h]) for h in range(2)]

    for copy in c_z2:
        copy.wait_recv()
    xj[eighth, :] = pair[...] + jnp.concatenate([y_z[2], y_z[3]], axis=0)
    c_xc, c_xy, forward_x = gather(xj, xy_s, xy_r, 5)

    for copy in c_r1:
        copy.wait_recv()
    r_sum[...] = r_part[chunk, :] + r_x[0] + (r_x[1] + r_x[2])
    c_r2 = []
    for d in (2, 1, 3):
        to = mod4(zl + d)
        c_r2.append(send(r_sum.at[rows(to * SHARD, SHARD), :], r_z.at[d - 1], r2_s.at[d - 1], r2_r.at[d - 1], at(zl=to)))

    c_g2 = []
    for h in range(2):
        c_g1[h].wait_recv()
        g_pair[small[h], :] = g_block[small[h], :] + g_zh[h]
        c_g2.append(send(g_pair.at[small[h], :], g_zh.at[2 + h], gh_s.at[2 + h], gh_r.at[2 + h], pairs[1 - h]))

    for copy in c_r2:
        copy.wait_recv()
    shard = rows(x * EIGHTH + zl * SHARD, SHARD)
    xr[shard, :] = dot3(split(r_sum[rows(zl * SHARD, SHARD), :] + r_z[0] + (r_z[1] + r_z[2])), t_pair, (1, 0))
    c_zl = [
        send(xr.at[shard, :], xr.at[shard, :], zl_s.at[d - 1], zl_r.at[d - 1], at(zl=mod4(zl + d))) for d in (2, 1, 3)
    ]


    for copy in c_g2:
        copy.wait_recv()
    g[mine32, :] = g_pair[...] + jnp.concatenate([g_zh[2], g_zh[3]], axis=0)
    c_ga = [
        send(g.at[mine32, :], g.at[mine32, :], ga_s.at[d - 1], ga_r.at[d - 1], at(x=mod4(x + d))) for d in (2, 1, 3)
    ]

    forward_x()
    for copy in c_zl:
        copy.wait_recv()
    c_rx = [
        send(xr.at[chunk, :], xr.at[chunk, :], rx_s.at[d - 1], rx_r.at[d - 1], at(x=mod4(x + d))) for d in (2, 1, 3)
    ]

    for copy in c_xc:
        copy.wait_recv()

    def first(n, carry):
        columns = rows(n * 256, 256)
        a[:, columns] -= dot3(p_pair, split(xj[columns, :]), (1, 1))
        return carry

    lax.fori_loop(0, 4, first, 0)
    for copy in c_ga:
        copy.wait_recv()
    c_gb = send(g.at[my64, :], g.at[my64, :], gc_s.at[1], gc_r.at[1], other)
    c_gb.wait_recv()
    q[...] = dot3(q_pair, split(g[...]), (1, 0))
    for copy in c_rx:
        copy.wait_recv()
    w_pair = split(xr[...] - q[...])

    def out(n):
        columns = rows(n * 256, 256)
        return pltpu.make_async_copy(a.at[:, columns], o_hbm.at[:, columns], store.at[n])

    def second(n, carry):
        columns = rows(n * 256, 256)
        a[:, columns] -= dot3(w_pair, (pj_high[columns, :], pj_low[columns, :]), (1, 1))
        out(n).start()
        return carry

    lax.fori_loop(0, 4, second, 0)
    for copy in [c_z, *c_y, *c_z1, *c_z2, *c_py, *c_pc, *c_gs, *c_xy, *c_zl, *c_gy, *c_rx, *c_gz, *c_xc, *c_ga, c_gc, c_gb, *c_r1, *c_r2, *c_g1, *c_g2]:
        copy.wait_send()
    for n in range(4):
        out(n).wait()


def per_device(matrix, panel, tfactor):
    dma = pltpu.SemaphoreType.DMA
    vmem = lambda *shape: pltpu.VMEM(shape, F32)
    return pl.pallas_call(
        kernel,
        out_shape=jax.ShapeDtypeStruct(matrix.shape, F32),
        in_specs=[pl.BlockSpec(memory_space=pltpu.HBM)] * 3,
        out_specs=pl.BlockSpec(memory_space=pl.ANY),
        scratch_shapes=[
            vmem(512, 1024), vmem(512, K), vmem(K, K),
            vmem(1024, K), vmem(512, K), vmem(3, EIGHTH, K), vmem(EIGHTH, K), vmem(EIGHTH, K), vmem(4, EIGHTH // 2, K),
            vmem(1024, K), vmem(1024, K), pltpu.VMEM((1024, K), BF16), pltpu.VMEM((1024, K), BF16),
            vmem(512, K), vmem(3, EIGHTH, K), vmem(EIGHTH, K), vmem(3, SHARD, K), vmem(512, K), vmem(512, K),
            vmem(K, K), vmem(128, K), vmem(3, SHARD, K), vmem(SHARD, K), vmem(3, SHARD, K), vmem(SHARD, K), vmem(3, SHARD, K),
            vmem(SHARD, K), vmem(4, SHARD // 2, K), vmem(SHARD, K), vmem(K, K),
            dma((3,)), dma((4,)), dma((9,)), dma((9,)), dma, dma, dma((3,)), dma((3,)), dma((3,)), dma((3,)),
            dma((4,)), dma((4,)), dma((3,)), dma((3,)), dma((3,)), dma((3,)), dma((3,)), dma((3,)),
            dma((3,)), dma((3,)), dma((3,)), dma((3,)), dma((7,)), dma((7,)), dma((3,)), dma((3,)),
            dma((3,)), dma((3,)), dma((4,)), dma((4,)), dma((7,)), dma((7,)), dma((2,)), dma((2,)),
        ],
        compiler_params=pltpu.CompilerParams(collective_id=0, has_side_effects=True, vmem_limit_bytes=62 * 2**20),
    )(matrix, panel, tfactor)


def solution(mesh):
    return jax.shard_map(
        per_device,
        mesh=mesh,
        in_specs=(P("row", "col"), P("row", None), P()),
        out_specs=P("row", "col"),
        check_vma=False,
    )
```
